128 devices in a mesh: req: 32 (over y, z, core), exp: 4 (over x).
Axes of the slice: x: 4, y: 4, z: 4, core: 2. Of those that a mesh axis runs over, the one named last changes fastest.
Arguments:
- queries: bfloat16 [64, 32, 6144], P('req', None, 'exp'), may hold values from -6 to 6
- cache_keys: bfloat16 [64, 512, 512], P('req', None, 'exp'), may hold values from -6 to 6
- cache_values: bfloat16 [64, 512, 512], P('req', None, 'exp'), may hold values from -6 to 6
- new_keys: bfloat16 [64, 32, 512], P('req', None, 'exp'), may hold values from -6 to 6
- new_values: bfloat16 [64, 32, 512], P('req', None, 'exp'), may hold values from -6 to 6
- counts: int32 [64], P('req'), may hold values from 1 to 32, as said below
- lengths: int32 [64], P('req'), may hold values from 2 to 512, as said below
- residual: bfloat16 [2048, 5120], P(('req', 'exp')), may hold values from -6 to 6
- o_weight: bfloat16 [6144, 5120], P('exp', 'req'), may hold values from -0.5 to 0.5
- norm_gain: float32 [5120], replicated, may hold values from 0.1 to 1.9
- expert_ids: int32 [2048, 8], P(('req', 'exp')), may hold values from 0 to 127, all different within a row; in each aligned block of 16 rows (0 to 15, 16 to 31, ...) at most 2 rows name the same one
- route_weights: float32 [2048, 8], P(('req', 'exp')), may hold values from 0.1 to 1
- gate_weight: bfloat16 [128, 5120, 768], P(('req', 'exp')), may hold values from -0.078125 to 0.078125
- up_weight: bfloat16 [128, 5120, 768], P(('req', 'exp')), may hold values from -0.078125 to 0.078125
- down_weight: bfloat16 [128, 768, 5120], P(('req', 'exp')), may hold values from -0.21875 to 0.21875
Outputs:
- mixed: bfloat16 [2048, 5120], P(('req', 'exp'))
The draws below stay inside these ranges and needn't reach their ends.
Inputs may be any that keep to these rules, and one draw needn't show every extreme that they name: `counts`: some request has exactly 32 forced tokens. `lengths`: some request has exactly 512 cached positions. `expert_ids`: each token slot names 8 different experts. Among the rows of one device (aligned blocks of 16 rows), at most 2 name one expert.
All inputs are finite; a program needn't handle non-finite values.
Results may differ from the reference program's by a relative error of at most 0.0075.
Values may be sent and summed in bfloat16 or wider, within the bound.
No kernel may reach another device: no remote copies, remote signals or barrier semaphores. Data moves between devices by JAX's collectives and lax.ppermute only.
A program may use at most 128 MiB of HBM per device.

```python
import math
import jax
import jax.numpy as jnp
import numpy as np
from jax import lax

D = 5120
HEADS = 48
KV_HEADS = 4
HEAD_DIM = 128
FF = 768
TOPK = 8
SLOTS = 32
CACHE = 512
REQS = 64
TOKENS = 2048
TQ = 16
EXPERTS = 128
CAP = 2


def draw_queries(key, part):
    key = jax.random.fold_in(key, 11)
    shape = (REQS, SLOTS, HEADS * HEAD_DIM)
    return jnp.clip(jax.random.normal(key, shape), -6.0, 6.0).astype(jnp.bfloat16)


def draw_cache_keys(key, part):
    key = jax.random.fold_in(key, 12)
    shape = (REQS, CACHE, KV_HEADS * HEAD_DIM)
    return jnp.clip(jax.random.normal(key, shape), -6.0, 6.0).astype(jnp.bfloat16)


def draw_counts(key, part):
    key = jax.random.fold_in(key, 21)
    first_key, second_key = jax.random.split(key)
    drawn_counts = jax.random.randint(first_key, (REQS,), 1, SLOTS + 1, dtype=jnp.int32)
    chosen_request = jax.random.randint(second_key, (), 0, REQS, dtype=jnp.int32)
    return jnp.where(jnp.arange(REQS, dtype=jnp.int32) == chosen_request, SLOTS, drawn_counts).astype(jnp.int32)


def draw_lengths(key, part):
    key = jax.random.fold_in(key, 22)
    first_key, second_key = jax.random.split(key)
    drawn_lengths = jax.random.randint(first_key, (REQS,), 2, CACHE + 1, dtype=jnp.int32)
    chosen_request = jax.random.randint(second_key, (), 0, REQS, dtype=jnp.int32)
    return jnp.where(jnp.arange(REQS, dtype=jnp.int32) == chosen_request, CACHE, drawn_lengths).astype(jnp.int32)


def block_levels(key, dims, pieces, least, largest):
    def one(axis_at, parts):
        steps = jax.random.uniform(jax.random.fold_in(jax.random.fold_in(key, 6), axis_at), (parts,), jnp.float32, least / len(pieces), largest / len(pieces))
        return jnp.repeat(jnp.exp(steps), dims[axis_at] // parts).reshape((-1,) + (1,) * (len(dims) - axis_at - 1))

    level = one(*pieces[0])
    for cut in pieces[1:]:
        level = level * one(*cut)
    return level


def routed_block(own_key, own, number, rows, count, top, bound, lean):
    ranking = jax.random.permutation(own_key, count)
    crowded, usual = portions_of(count, rows * top, bound, lean, True), portions_of(count, rows * top, bound, lean, False)
    places = jnp.arange(count)

    def named(tallies, rotation):
        used = int((tallies > 0).sum())
        fixed = max(1, used // 4)
        passed = fixed + (places - fixed + rotation * (used - fixed)) % max(1, count - fixed)
        return jnp.zeros((count,), jnp.int32).at[ranking[jnp.where(places < fixed, places, passed)]].set(jnp.asarray(tallies, jnp.int32))

    tallies = jnp.where(number % 4 == 0, named(crowded, number // 4), named(usual, number - number // 4 - 1))
    mixed = jax.random.permutation(jax.random.fold_in(own, 3), count)
    donor, taker = mixed[0:count // 2 * 2:2], mixed[1:count // 2 * 2:2]
    slack = jnp.minimum(tallies[donor] - 1, bound - tallies[taker]) // 2
    slack = jnp.where((donor == ranking[0]) | (taker == ranking[0]) | (tallies[taker] == 0), 0, jnp.maximum(slack, 0))
    passed = jax.random.randint(jax.random.fold_in(own, 4), (count // 2,), 0, 1 << 20) % (slack + 1)
    tallies = tallies.at[donor].add(-passed).at[taker].add(passed)
    items = jnp.searchsorted(jnp.cumsum(tallies), jnp.arange(rows * top), side="right").astype(jnp.int32)
    grid = items.reshape(top, rows).T
    grid = grid[jax.random.permutation(jax.random.fold_in(own, 1), rows)]
    rotation = jax.random.randint(jax.random.fold_in(own, 2), (rows, 1), 0, top)
    return jnp.take_along_axis(grid, (jnp.arange(top)[None, :] + rotation) % top, axis=1)


def portions_of(number_of, total, bound, slope, full):
    portions = [(1 << 20) // math.isqrt(grade ** slope) + 1 for grade in range(1, number_of + 1)]
    largest = bound if full else min(bound, max(-(-total // number_of), total * portions[0] // sum(portions)))
    least = 1 if total - largest >= number_of - 1 else 0
    holding, rest = [largest] + [least] * (number_of - 1), total - largest - least * (number_of - 1)
    while rest > 0:
        movable = [i for i in range(1, number_of) if holding[i] < largest] or [i for i in range(1, number_of) if holding[i] < bound]
        whole, remaining = sum([portions[i] for i in movable]), rest
        for i in movable:
            extra = min(bound - holding[i], max(1, remaining * portions[i] // whole), rest)
            holding[i] = holding[i] + extra
            rest = rest - extra
    return np.array(holding)


def bell_draw(own_key, shape, spread, reach, cuts=(), kind=jnp.bfloat16):
    level = block_levels(own_key, shape, cuts, -0.22, 0.18) if cuts else 1.0
    values = jax.random.normal(own_key, shape, jnp.float32) * spread * level
    return jnp.minimum(jnp.maximum(values, -reach), reach).astype(kind)


def setup_inputs(seed: int = 0) -> dict:
    key_of = jax.random.split(jax.random.key(seed), 16)
    queries = draw_queries(jax.random.fold_in(key_of[15], 71), 0)
    cache_keys = draw_cache_keys(jax.random.fold_in(key_of[15], 71), 0)
    cache_values = bell_draw(key_of[2], (REQS, CACHE, KV_HEADS * HEAD_DIM), 1.0, 6.0, ((0, 32), (2, 4)))
    new_keys = bell_draw(key_of[3], (REQS, SLOTS, KV_HEADS * HEAD_DIM), 1.0, 6.0, ((0, 32), (2, 4)))
    new_values = bell_draw(key_of[4], (REQS, SLOTS, KV_HEADS * HEAD_DIM), 1.0, 6.0, ((0, 32), (2, 4)))
    counts = draw_counts(jax.random.fold_in(key_of[15], 71), 0)
    lengths = draw_lengths(jax.random.fold_in(key_of[15], 71), 0)
    residual = bell_draw(key_of[7], (TOKENS, D), 1.0, 6.0, ((0, 128),))
    o_weight = bell_draw(key_of[8], (HEADS * HEAD_DIM, D), HEAD_DIM ** -0.5, 0.5, ((0, 4), (1, 32)))
    norm_gain = jnp.clip(1.0 + 0.18 * jax.random.normal(key_of[9], (D,), jnp.float32), 0.1, 1.9)
    expert_ids_keys = jax.random.split(jax.random.fold_in(key_of[10], 1), TOKENS // TQ)
    expert_ids_turns = jax.random.permutation(jax.random.fold_in(key_of[10], 3), TOKENS // TQ)
    expert_ids = jax.vmap(lambda own, number: routed_block(jax.random.fold_in(key_of[10], 2), own, number, TQ, EXPERTS, TOPK, CAP, 2))(expert_ids_keys, expert_ids_turns).reshape((TOKENS, TOPK))
    route_weights = jnp.clip(jnp.exp(math.log(1.0) - 2.3025851 * jax.random.uniform(key_of[11], (TOKENS, TOPK), jnp.float32) ** block_levels(key_of[11], (TOKENS, TOPK), ((0, 128),), -0.2, 0.2)), 0.1, 1.0)
    gate_weight = bell_draw(key_of[12], (EXPERTS, D, FF), D ** -0.5, 0.078125, ((0, 128),))
    up_weight = bell_draw(key_of[13], (EXPERTS, D, FF), D ** -0.5, 0.078125, ((0, 128),))
    down_weight = bell_draw(key_of[14], (EXPERTS, FF, D), FF ** -0.5, 0.21875, ((0, 128),))
    return dict(queries=queries, cache_keys=cache_keys, cache_values=cache_values, new_keys=new_keys, new_values=new_values, counts=counts, lengths=lengths, residual=residual, o_weight=o_weight, norm_gain=norm_gain, expert_ids=expert_ids, route_weights=route_weights, gate_weight=gate_weight, up_weight=up_weight, down_weight=down_weight)


def visible(slot_count, cached, counts, lengths):
    position = jnp.arange(cached + slot_count, dtype=jnp.int32)
    fresh_index = position - cached
    slot_index = jnp.arange(slot_count, dtype=jnp.int32)
    cache_ok = position[None, None, :] < lengths[:, None, None]
    newer_ok = (fresh_index[None, None, :] <= slot_index[None, :, None]) & (fresh_index[None, None, :] < counts[:, None, None])
    return jnp.where(position[None, None, :] < cached, cache_ok, newer_ok)

def attend(queries, cache_keys, cache_values, new_keys, new_values, counts, lengths):
    requests, slot_count, head_width = queries.shape
    cached = cache_keys.shape[1]
    key_heads = cache_keys.shape[2] // HEAD_DIM
    grouped = head_width // (key_heads * HEAD_DIM)
    query_heads = queries.astype(jnp.float32).reshape(requests, slot_count, key_heads, grouped, HEAD_DIM)
    keys_joined = jnp.concatenate([cache_keys, new_keys], axis=1).astype(jnp.float32).reshape(requests, cached + slot_count, key_heads, HEAD_DIM)
    values_joined = jnp.concatenate([cache_values, new_values], axis=1).astype(jnp.float32).reshape(requests, cached + slot_count, key_heads, HEAD_DIM)
    scores = jnp.einsum('rskgd,rpkd->rkgsp', query_heads, keys_joined) / math.sqrt(HEAD_DIM)
    allowed = visible(slot_count, cached, counts, lengths)
    scores = jnp.where(allowed[:, None, None], scores, -jnp.inf)
    highest = lax.optimization_barrier(jnp.max(scores, axis=-1, keepdims=True))
    exponentials = jnp.exp(scores - highest)
    probabilities = (exponentials / lax.optimization_barrier(jnp.sum(exponentials, axis=-1, keepdims=True))).astype(jnp.bfloat16)
    mixed_heads = jnp.einsum('rkgsp,rpkd->rskgd', probabilities.astype(jnp.float32), values_joined)
    return mixed_heads.reshape(requests, slot_count, head_width).astype(jnp.bfloat16)

def scale_rows(hidden_state, norm_gain):
    mean_square = lax.optimization_barrier(jnp.mean(hidden_state * hidden_state, axis=-1, keepdims=True))
    return (hidden_state * lax.rsqrt(mean_square + 1e-05) * norm_gain.astype(jnp.float32)).astype(jnp.bfloat16)

def expert_apply(token_rows, gate_matrix, up_matrix, down_matrix):
    gate_part = jnp.dot(token_rows, gate_matrix, preferred_element_type=jnp.float32)
    up_part = jnp.dot(token_rows, up_matrix, preferred_element_type=jnp.float32)
    inner = (jax.nn.silu(gate_part) * up_part).astype(jnp.bfloat16)
    return jnp.dot(inner, down_matrix, preferred_element_type=jnp.float32).astype(jnp.bfloat16)

def reference(queries, cache_keys, cache_values, new_keys, new_values, counts, lengths, residual, o_weight, norm_gain, expert_ids, route_weights, gate_weight, up_weight, down_weight):
    attended = attend(queries, cache_keys, cache_values, new_keys, new_values, counts, lengths).reshape(TOKENS, HEADS * HEAD_DIM)
    projected = jnp.dot(attended, o_weight, preferred_element_type=jnp.float32)
    hidden_state = residual.astype(jnp.float32) + projected
    normed = scale_rows(hidden_state, norm_gain)
    flat_ids = expert_ids.reshape(-1)
    flat_weights = route_weights.reshape(-1)
    bound_rows = EXPERTS * CAP

    def one_expert(running, expert):
        chosen = flat_ids == expert
        picked = jnp.nonzero(chosen, size=bound_rows, fill_value=0)[0].astype(jnp.int32)
        filled = jnp.arange(bound_rows, dtype=jnp.int32) < jnp.sum(chosen.astype(jnp.int32))
        token_rows = picked // TOPK
        outputs = expert_apply(normed[token_rows], gate_weight[expert], up_weight[expert], down_weight[expert])
        scaled = outputs.astype(jnp.float32) * jnp.where(filled, flat_weights[picked], 0.0)[:, None]
        return (running.at[token_rows].add(scaled), None)
    combined, _ = lax.scan(one_expert, jnp.zeros((TOKENS, D), jnp.float32), jnp.arange(EXPERTS, dtype=jnp.int32))
    slot_index = jnp.arange(TOKENS, dtype=jnp.int32) % SLOTS
    live_rows = slot_index < jnp.repeat(counts, SLOTS)
    return jnp.where(live_rows[:, None], hidden_state + combined, 0.0).astype(jnp.bfloat16)
```

```python
import math

import jax
import jax.numpy as jnp
from jax import lax
from jax.experimental import pallas as pl
from jax.experimental.pallas import tpu as pltpu
from jax.sharding import Mesh
from jax.sharding import PartitionSpec as P

HEAD_DIM = 128
TOPK = 8
CAP = 2
LANES = 128
SEG = 8
AXES = ("y", "z", "c", "x")
BF = jnp.bfloat16
F32 = jnp.float32


def dot(a, b):
    return jnp.dot(a, b, preferred_element_type=F32)


def dot_t(a, b):
    return lax.dot_general(a, b, (((1,), (1,)), ((), ())), preferred_element_type=F32)


def vmem(n):
    return [pl.BlockSpec(memory_space=pltpu.VMEM)] * n


def attend_kernel(counts, lengths, q_ref, k_ref, v_ref, nk_ref, nv_ref, out_ref):
    requests, slots, width = q_ref.shape
    heads = width // HEAD_DIM
    cached = k_ref.shape[1]
    rows = heads * slots
    scale = 1.0 / math.sqrt(HEAD_DIM)
    slot = lax.broadcasted_iota(jnp.int32, (rows, slots), 0) % slots
    fresh = lax.broadcasted_iota(jnp.int32, (rows, slots), 1)
    position = lax.broadcasted_iota(jnp.int32, (rows, cached), 1)
    for r in range(requests):
        q = jnp.concatenate(
            [q_ref[r, :, h * HEAD_DIM : (h + 1) * HEAD_DIM] for h in range(heads)], axis=0
        )
        old = dot_t(q, k_ref[r]) * scale
        new = dot_t(q, nk_ref[r]) * scale
        old = jnp.where(position < lengths[r], old, -1e30)
        new = jnp.where((fresh <= slot) & (fresh < counts[r]), new, -1e30)
        highest = jnp.maximum(
            jnp.max(old, axis=1, keepdims=True), jnp.max(new, axis=1, keepdims=True)
        )
        old = jnp.exp(old - highest)
        new = jnp.exp(new - highest)
        total = jnp.sum(old, axis=1, keepdims=True) + jnp.sum(new, axis=1, keepdims=True)
        inverse = 1.0 / total
        mixed = dot((old * inverse).astype(BF), v_ref[r]) + dot(
            (new * inverse).astype(BF), nv_ref[r]
        )
        mixed = mixed.astype(BF)
        for h in range(heads):
            out_ref[r * slots : (r + 1) * slots, h * HEAD_DIM : (h + 1) * HEAD_DIM] = mixed[
                h * slots : (h + 1) * slots
            ]


def attend(queries, cache_keys, cache_values, new_keys, new_values, counts, lengths):
    requests, slots, width = queries.shape
    return pl.pallas_call(
        attend_kernel,
        out_shape=jax.ShapeDtypeStruct((requests * slots, width), BF),
        in_specs=[pl.BlockSpec(memory_space=pltpu.SMEM)] * 2 + vmem(5),
        out_specs=pl.BlockSpec(memory_space=pltpu.VMEM),
        compiler_params=pltpu.CompilerParams(vmem_limit_bytes=32 << 20),
        cost_estimate=pl.CostEstimate(
            flops=4 * 768 * 544 * 128, bytes_accessed=1 << 20, transcendentals=768 * 544
        ),
        name="attend",
    )(counts, lengths, queries, cache_keys, cache_values, new_keys, new_values)


def norm_kernel(arrived_ref, residual_ref, gain_ref, place_ref, hidden_ref, out_ref):
    blocks, rows, part = arrived_ref.shape
    width = residual_ref.shape[1]
    groups = width // part
    splits = blocks // groups
    square = jnp.zeros((rows, 1), F32)
    for g in range(groups):
        total = residual_ref[:, g * part : (g + 1) * part].astype(F32)
        for k in range(splits):
            total = total + arrived_ref[g * splits + k].astype(F32)
        hidden_ref[:, g * part : (g + 1) * part] = total
        square = square + jnp.sum(total * total, axis=1, keepdims=True)
    factor = lax.rsqrt(square / width + 1e-05)
    seg = width // SEG
    normed = jnp.concatenate(
        [
            (
                hidden_ref[:, s * seg : (s + 1) * seg]
                * factor
                * gain_ref[:, s * seg : (s + 1) * seg]
            ).astype(BF)
            for s in range(SEG)
        ],
        axis=0,
    )
    tile = 256
    for i in range(out_ref.shape[0] // tile):
        at = pl.ds(i * tile, tile)
        out_ref[at, :] = dot(place_ref[at, :], normed).astype(BF)


def norm_and_place(arrived, residual, gain, place):
    rows, width = residual.shape
    return pl.pallas_call(
        norm_kernel,
        out_shape=(
            jax.ShapeDtypeStruct((rows, width), F32),
            jax.ShapeDtypeStruct((place.shape[0], width // SEG), BF),
        ),
        in_specs=vmem(4),
        out_specs=tuple(vmem(2)),
        compiler_params=pltpu.CompilerParams(vmem_limit_bytes=32 << 20),
        name="norm_place",
    )(arrived, residual, gain, place)


def expert_kernel(
    x_ref, gate_hbm, up_hbm, down_hbm, out_ref, stage, gate, up, down, inner, sems
):
    rows = x_ref.shape[0] // SEG
    seg = x_ref.shape[1]
    half = gate.shape[1]
    lanes = seg // LANES

    def piece(kind, s):
        at = pl.ds(s * seg, seg)
        if kind == 0:
            return pltpu.make_async_copy(gate_hbm.at[at, :], gate.at[at, :], sems.at[0, s])
        if kind == 1:
            return pltpu.make_async_copy(up_hbm.at[at, :], up.at[at, :], sems.at[1, s])
        return pltpu.make_async_copy(down_hbm.at[:, at], down.at[:, at], sems.at[2, s])

    for s in range(SEG):
        piece(0, s).start()
        piece(1, s).start()
    for s in range(SEG):
        piece(2, s).start()
    tile = 256
    for i in range(x_ref.shape[0] // tile):
        at = pl.ds(i * tile, tile)
        for k in range(lanes):
            stage[k, at, :] = x_ref[at, k * LANES : (k + 1) * LANES].astype(F32)
    gate_sum = jnp.zeros((rows, half), F32)
    up_sum = jnp.zeros((rows, half), F32)
    for s in range(SEG):
        x = jnp.concatenate(
            [stage[k, pl.ds(s, rows, stride=SEG), :].astype(BF) for k in range(lanes)], axis=1
        )
        piece(0, s).wait()
        gate_sum = gate_sum + dot(x, gate[pl.ds(s * seg, seg), :])
        piece(1, s).wait()
        up_sum = up_sum + dot(x, up[pl.ds(s * seg, seg), :])
    inner[...] = (gate_sum / (1.0 + jnp.exp(-gate_sum)) * up_sum).astype(BF)
    for s in range(SEG):
        piece(2, s).wait()
        result = dot(inner[...], down[:, pl.ds(s * seg, seg)])
        for k in range(lanes):
            stage[k, pl.ds(s, rows, stride=SEG), :] = result[:, k * LANES : (k + 1) * LANES]
    for i in range(x_ref.shape[0] // tile):
        at = pl.ds(i * tile, tile)
        for k in range(lanes):
            out_ref[at, k * LANES : (k + 1) * LANES] = stage[k, at, :].astype(BF)


def apply_expert(rows, gate, up, down):
    count, seg = rows.shape
    width, half = gate.shape
    return pl.pallas_call(
        expert_kernel,
        out_shape=jax.ShapeDtypeStruct((count, seg), BF),
        in_specs=vmem(1) + [pl.BlockSpec(memory_space=pl.ANY)] * 3,
        out_specs=pl.BlockSpec(memory_space=pltpu.VMEM),
        scratch_shapes=[
            pltpu.VMEM((seg // LANES, count, LANES), F32),
            pltpu.VMEM((width, half), BF),
            pltpu.VMEM((width, half), BF),
            pltpu.VMEM((half, width), BF),
            pltpu.VMEM((count // SEG, half), BF),
            pltpu.SemaphoreType.DMA((3, SEG)),
        ],
        compiler_params=pltpu.CompilerParams(vmem_limit_bytes=52 << 20),
        name="expert",
    )(rows, gate, up, down)


def combine_kernel(back_ref, high_ref, low_ref, hidden_ref, live_ref, out_ref):
    rows, width = hidden_ref.shape
    seg = width // SEG
    back = back_ref[...]
    mixed = dot(high_ref[...], back) + dot(low_ref[...], back)
    live = live_ref[...] > 0
    for s in range(SEG):
        at = slice(s * seg, (s + 1) * seg)
        total = hidden_ref[:, at] + mixed[s * rows : (s + 1) * rows]
        out_ref[:, at] = jnp.where(live, total, 0.0).astype(BF)


def combine(back, high, low, hidden, live):
    return pl.pallas_call(
        combine_kernel,
        out_shape=jax.ShapeDtypeStruct(hidden.shape, BF),
        in_specs=vmem(5),
        out_specs=pl.BlockSpec(memory_space=pltpu.VMEM),
        compiler_params=pltpu.CompilerParams(vmem_limit_bytes=32 << 20),
        name="combine",
    )(back, high, low, hidden, live)


def routing(expert_ids, route_weights, experts):
    tokens = expert_ids.shape[0]
    pairs = tokens * TOPK
    destination = expert_ids.reshape(pairs)
    number = jnp.arange(pairs, dtype=jnp.int32)
    earlier = (destination[:, None] == destination[None, :]) & (number[:, None] < number[None, :])
    rank = jnp.sum(earlier.astype(jnp.int32), axis=0)
    slot = destination * CAP + rank
    match = slot[None, :] == jnp.arange(experts * CAP, dtype=jnp.int32)[:, None]
    token = jnp.sum(jnp.where(match, number[None, :] // TOPK + 1, 0), axis=1) - 1
    weight = jnp.sum(jnp.where(match, route_weights.reshape(pairs)[None, :], 0.0), axis=1)
    line = jnp.arange(experts * CAP * SEG, dtype=jnp.int32)
    token_line = jnp.repeat(token, SEG)
    key = jnp.where(token_line < 0, -1, (line % SEG) * tokens + token_line)
    weight_line = jnp.repeat(weight, SEG)
    spot = jnp.arange(SEG * tokens, dtype=jnp.int32)
    place = (key[:, None] == spot[None, :]).astype(BF)
    high = lax.reduce_precision(weight_line, 8, 7)
    low = weight_line - high
    here = spot[:, None] == key[None, :]
    return (
        place,
        jnp.where(here, high[None, :], 0.0).astype(BF),
        jnp.where(here, low[None, :], 0.0).astype(BF),
    )


def per_device(
    queries,
    cache_keys,
    cache_values,
    new_keys,
    new_values,
    counts,
    lengths,
    residual,
    o_weight,
    norm_gain,
    expert_ids,
    route_weights,
    gate_weight,
    up_weight,
    down_weight,
):
    requests, slots, _ = queries.shape
    rows, width = residual.shape
    experts = math.prod(lax.axis_size(a) for a in AXES)
    weight = lax.all_gather(o_weight.T, ("z", "c"), axis=0, tiled=True)
    attended = attend(queries, cache_keys, cache_values, new_keys, new_values, counts, lengths)
    tokens = lax.all_gather(attended, "y", axis=0, tiled=True)
    place, high, low = routing(expert_ids, route_weights, experts)
    token_index = lax.axis_index("x") * rows + jnp.arange(rows, dtype=jnp.int32)
    count_of = jnp.sum(
        jnp.where(
            (token_index // slots)[:, None] == jnp.arange(requests, dtype=jnp.int32)[None, :],
            counts[None, :],
            0,
        ),
        axis=1,
    )
    live = (token_index % slots < count_of).astype(jnp.int32)[:, None]
    partial = dot_t(tokens, weight).astype(BF)
    partial = partial.reshape(-1, rows, partial.shape[1])
    arrived = lax.all_to_all(partial, ("y", "x"), split_axis=0, concat_axis=0, tiled=True)
    hidden, outgoing = norm_and_place(arrived, residual, norm_gain[None, :], place)
    outgoing = outgoing.reshape(experts, CAP * SEG, width // SEG)
    received = lax.all_to_all(outgoing, AXES, split_axis=0, concat_axis=0, tiled=True)
    results = apply_expert(
        received.reshape(-1, width // SEG), gate_weight[0], up_weight[0], down_weight[0]
    )
    results = results.reshape(experts, CAP * SEG, width // SEG)
    back = lax.all_to_all(results, AXES, split_axis=0, concat_axis=0, tiled=True)
    return combine(back.reshape(-1, width // SEG), high, low, hidden, live)


def solution(mesh):
    fine = Mesh(mesh.devices.reshape(4, 4, 2, 4), AXES)
    req = ("y", "z", "c")
    every = AXES
    return jax.shard_map(
        per_device,
        mesh=fine,
        in_specs=(
            P(req, None, "x"),
            P(req, None, "x"),
            P(req, None, "x"),
            P(req, None, "x"),
            P(req, None, "x"),
            P(req),
            P(req),
            P(every, None),
            P("x", req),
            P(),
            P(every, None),
            P(every, None),
            P(every, None, None),
            P(every, None, None),
            P(every, None, None),
        ),
        out_specs=P(every, None),
        check_vma=False,
    )
```

```python
import math

import jax
import jax.numpy as jnp
from jax import lax
from jax.experimental import pallas as pl
from jax.experimental.pallas import tpu as pltpu
from jax.sharding import Mesh
from jax.sharding import PartitionSpec as P

HEAD_DIM = 128
TOPK = 8
CAP = 2
LANES = 128
AHEAD = 6
SEG = 4
AXES = ("y", "z", "c", "x")
BF = jnp.bfloat16
F32 = jnp.float32


def dot(a, b):
    return jnp.dot(a, b, preferred_element_type=F32)


def dot_t(a, b):
    return lax.dot_general(a, b, (((1,), (1,)), ((), ())), preferred_element_type=F32)


def vmem(n):
    return [pl.BlockSpec(memory_space=pltpu.VMEM)] * n


def attend_kernel(
    counts_hbm,
    lengths_hbm,
    q_hbm,
    k_hbm,
    v_hbm,
    nk_hbm,
    nv_hbm,
    out_ref,
    counts,
    lengths,
    q_ref,
    k_ref,
    v_ref,
    nk_ref,
    nv_ref,
    sems,
):
    pairs = (
        (q_hbm, q_ref),
        (k_hbm, k_ref),
        (nk_hbm, nk_ref),
        (lengths_hbm, lengths),
        (counts_hbm, counts),
        (v_hbm, v_ref),
        (nv_hbm, nv_ref),
    )
    copies = [pltpu.make_async_copy(a, b, sems.at[i]) for i, (a, b) in enumerate(pairs)]
    for copy in copies:
        copy.start()
    requests, slots, width = q_ref.shape
    heads = width // HEAD_DIM
    cached = k_ref.shape[1]
    rows = heads * slots
    scale = 1.0 / math.sqrt(HEAD_DIM)
    slot = lax.broadcasted_iota(jnp.int32, (rows, slots), 0) % slots
    fresh = lax.broadcasted_iota(jnp.int32, (rows, slots), 1)
    position = lax.broadcasted_iota(jnp.int32, (rows, cached), 1)
    for copy in copies:
        copy.wait()
    for r in range(requests):
        q = jnp.concatenate(
            [q_ref[r, :, h * HEAD_DIM : (h + 1) * HEAD_DIM] for h in range(heads)], axis=0
        )
        old = dot_t(q, k_ref[r]) * scale
        new = dot_t(q, nk_ref[r]) * scale
        old = jnp.where(position < lengths[r], old, -1e30)
        new = jnp.where((fresh <= slot) & (fresh < counts[r]), new, -1e30)
        highest = jnp.maximum(
            jnp.max(old, axis=1, keepdims=True), jnp.max(new, axis=1, keepdims=True)
        )
        old = jnp.exp(old - highest)
        new = jnp.exp(new - highest)
        total = jnp.sum(old, axis=1, keepdims=True) + jnp.sum(new, axis=1, keepdims=True)
        inverse = 1.0 / total
        mixed = dot((old * inverse).astype(BF), v_ref[r]) + dot(
            (new * inverse).astype(BF), nv_ref[r]
        )
        mixed = mixed.astype(BF)
        for h in range(heads):
            out_ref[r * slots : (r + 1) * slots, h * HEAD_DIM : (h + 1) * HEAD_DIM] = mixed[
                h * slots : (h + 1) * slots
            ]


def attend(queries, cache_keys, cache_values, new_keys, new_values, counts, lengths):
    requests, slots, width = queries.shape
    arrays = (queries, cache_keys, cache_values, new_keys, new_values)
    return pl.pallas_call(
        attend_kernel,
        out_shape=jax.ShapeDtypeStruct((requests * slots, width), BF),
        in_specs=[pl.BlockSpec(memory_space=pl.ANY)] * 7,
        out_specs=pl.BlockSpec(memory_space=pltpu.VMEM),
        scratch_shapes=[pltpu.SMEM((requests,), jnp.int32)] * 2
        + [pltpu.VMEM(a.shape, a.dtype) for a in arrays]
        + [pltpu.SemaphoreType.DMA((7,))],
        compiler_params=pltpu.CompilerParams(vmem_limit_bytes=60 << 20),
        cost_estimate=pl.CostEstimate(
            flops=4 * 768 * 544 * 128, bytes_accessed=1 << 20, transcendentals=768 * 544
        ),
        name="attend",
    )(counts, lengths, *arrays)


def project_kernel(tokens_hbm, *refs):
    pieces, (out_ref, tokens, weight, sems) = refs[:-4], refs[-4:]
    zs, cs = lax.axis_size("z"), lax.axis_size("c")
    z, c = lax.axis_index("z"), lax.axis_index("c")
    part = pieces[0].shape[0]
    copies = [pltpu.make_async_copy(tokens_hbm, tokens, sems.at[zs * cs])]
    for i, piece in enumerate(pieces):
        home = lax.rem(z + zs - i // cs, zs) * cs + lax.rem(c + i, cs)
        at = pl.ds(pl.multiple_of(home * part, part), part)
        copies.append(pltpu.make_async_copy(piece, weight.at[at, :], sems.at[i]))
    for copy in copies:
        copy.start()
    for copy in copies:
        copy.wait()
    tile = 256
    for j in range(out_ref.shape[1] // tile):
        at = slice(j * tile, (j + 1) * tile)
        out_ref[:, at] = dot_t(tokens[...], weight[at, :]).astype(BF)


def project(tokens, o_weight, ready):
    zs = lax.axis_size("z")
    swap = [(0, 1), (1, 0)]
    own = o_weight.T
    along = [own] + [
        lax.ppermute(own, "z", [(i, (i + k) % zs) for i in range(zs)]) for k in range(1, zs)
    ]
    *along, tokens, ready = lax.optimization_barrier((*along, tokens, ready))
    pieces = []
    for piece in along:
        pieces += [piece, lax.ppermute(piece, "c", swap)]
    part, depth = own.shape
    columns = part * len(pieces)
    call = pl.pallas_call(
        project_kernel,
        out_shape=jax.ShapeDtypeStruct((tokens.shape[0], columns), BF),
        in_specs=[pl.BlockSpec(memory_space=pl.ANY)] * (1 + len(pieces)),
        out_specs=pl.BlockSpec(memory_space=pltpu.VMEM),
        scratch_shapes=[
            pltpu.VMEM(tokens.shape, BF),
            pltpu.VMEM((columns, depth), BF),
            pltpu.SemaphoreType.DMA((len(pieces) + 1,)),
        ],
        compiler_params=pltpu.CompilerParams(vmem_limit_bytes=60 << 20),
        name="project",
    )
    return call(tokens, *pieces), ready


def norm_kernel(arrived_ref, residual_ref, gain_ref, place_ref, hidden_ref, out_ref):
    blocks, rows, part = arrived_ref.shape
    width = residual_ref.shape[1]
    groups = width // part
    splits = blocks // groups
    square = jnp.zeros((rows, 1), F32)
    for g in range(groups):
        total = residual_ref[:, g * part : (g + 1) * part].astype(F32)
        for k in range(splits):
            total = total + arrived_ref[g * splits + k].astype(F32)
        hidden_ref[:, g * part : (g + 1) * part] = total
        square = square + jnp.sum(total * total, axis=1, keepdims=True)
    factor = lax.rsqrt(square / width + 1e-05)
    seg = width // SEG
    normed = jnp.concatenate(
        [
            (
                hidden_ref[:, s * seg : (s + 1) * seg]
                * factor
                * gain_ref[:, s * seg : (s + 1) * seg]
            ).astype(BF)
            for s in range(SEG)
        ],
        axis=0,
    )
    tile = 256
    for i in range(out_ref.shape[0] // tile):
        at = pl.ds(i * tile, tile)
        out_ref[at, :] = dot(place_ref[at, :], normed).astype(BF)


def norm_and_place(arrived, residual, gain, place):
    rows, width = residual.shape
    return pl.pallas_call(
        norm_kernel,
        out_shape=(
            jax.ShapeDtypeStruct((rows, width), F32),
            jax.ShapeDtypeStruct((place.shape[0], width // SEG), BF),
        ),
        in_specs=vmem(4),
        out_specs=tuple(vmem(2)),
        compiler_params=pltpu.CompilerParams(vmem_limit_bytes=32 << 20),
        name="norm_place",
    )(arrived, residual, gain, place)


def expert_kernel(
    x_ref, gate_hbm, up_hbm, down_hbm, out_ref, stage, inner, gate, up, down, sems
):
    rows = x_ref.shape[0] // SEG
    seg = x_ref.shape[1]
    lanes = seg // LANES
    copies = []
    for s in range(SEG):
        at = pl.ds(s * seg, seg)
        copies.append(pltpu.make_async_copy(gate_hbm.at[at, :], gate.at[at, :], sems.at[0, s]))
        copies.append(pltpu.make_async_copy(up_hbm.at[at, :], up.at[at, :], sems.at[1, s]))
    for s in range(SEG):
        at = pl.ds(s * seg, seg)
        copies.append(pltpu.make_async_copy(down_hbm.at[:, at], down.at[:, at], sems.at[2, s]))

    def need(i):
        copies[i].wait()
        if i + AHEAD < len(copies):
            copies[i + AHEAD].start()

    for copy in copies[:AHEAD]:
        copy.start()
    tile = 256
    for i in range(x_ref.shape[0] // tile):
        at = pl.ds(i * tile, tile)
        for k in range(lanes):
            stage[k, at, :] = x_ref[at, k * LANES : (k + 1) * LANES].astype(F32)
    gate_sum = up_sum = None
    for s in range(SEG):
        at = pl.ds(s * seg, seg)
        x = jnp.concatenate(
            [stage[k, pl.ds(s, rows, stride=SEG), :].astype(BF) for k in range(lanes)], axis=1
        )
        need(2 * s)
        gate_part = dot(x, gate[at, :])
        need(2 * s + 1)
        up_part = dot(x, up[at, :])
        gate_sum = gate_part if s == 0 else gate_sum + gate_part
        up_sum = up_part if s == 0 else up_sum + up_part
    inner[...] = (gate_sum / (1.0 + jnp.exp(-gate_sum)) * up_sum).astype(BF)
    for s in range(SEG):
        need(2 * SEG + s)
        result = dot(inner[...], down[:, pl.ds(s * seg, seg)])
        for k in range(lanes):
            stage[k, pl.ds(s, rows, stride=SEG), :] = result[:, k * LANES : (k + 1) * LANES]
    for i in range(x_ref.shape[0] // tile):
        at = pl.ds(i * tile, tile)
        for k in range(lanes):
            out_ref[at, k * LANES : (k + 1) * LANES] = stage[k, at, :].astype(BF)


def apply_expert(rows, gate, up, down):
    count, seg = rows.shape
    width, half = gate.shape
    return pl.pallas_call(
        expert_kernel,
        out_shape=jax.ShapeDtypeStruct((count, seg), BF),
        in_specs=vmem(1) + [pl.BlockSpec(memory_space=pl.ANY)] * 3,
        out_specs=pl.BlockSpec(memory_space=pltpu.VMEM),
        scratch_shapes=[
            pltpu.VMEM((seg // LANES, count, LANES), F32),
            pltpu.VMEM((count // SEG, half), BF),
            pltpu.VMEM((width, half), BF),
            pltpu.VMEM((width, half), BF),
            pltpu.VMEM((half, width), BF),
            pltpu.SemaphoreType.DMA((3, SEG)),
        ],
        compiler_params=pltpu.CompilerParams(vmem_limit_bytes=44 << 20),
        name="expert",
    )(rows, gate, up, down)


def combine_kernel(back_ref, high_ref, low_ref, hidden_ref, live_ref, out_ref):
    rows, width = hidden_ref.shape
    seg = width // SEG
    back = back_ref[...]
    mixed = dot(high_ref[...], back) + dot(low_ref[...], back)
    live = live_ref[...] > 0
    for s in range(SEG):
        at = slice(s * seg, (s + 1) * seg)
        total = hidden_ref[:, at] + mixed[s * rows : (s + 1) * rows]
        out_ref[:, at] = jnp.where(live, total, 0.0).astype(BF)


def combine(back, high, low, hidden, live):
    return pl.pallas_call(
        combine_kernel,
        out_shape=jax.ShapeDtypeStruct(hidden.shape, BF),
        in_specs=vmem(5),
        out_specs=pl.BlockSpec(memory_space=pltpu.VMEM),
        compiler_params=pltpu.CompilerParams(vmem_limit_bytes=32 << 20),
        name="combine",
    )(back, high, low, hidden, live)


def routing(expert_ids, route_weights, experts):
    tokens = expert_ids.shape[0]
    pairs = tokens * TOPK
    destination = expert_ids.reshape(pairs)
    number = jnp.arange(pairs, dtype=jnp.int32)
    earlier = (destination[:, None] == destination[None, :]) & (number[:, None] < number[None, :])
    rank = jnp.sum(earlier.astype(jnp.int32), axis=0)
    slot = destination * CAP + rank
    match = slot[None, :] == jnp.arange(experts * CAP, dtype=jnp.int32)[:, None]
    token = jnp.sum(jnp.where(match, number[None, :] // TOPK + 1, 0), axis=1) - 1
    weight = jnp.sum(jnp.where(match, route_weights.reshape(pairs)[None, :], 0.0), axis=1)
    line = jnp.arange(experts * CAP * SEG, dtype=jnp.int32)
    token_line = jnp.repeat(token, SEG)
    key = jnp.where(token_line < 0, -1, (line % SEG) * tokens + token_line)
    weight_line = jnp.repeat(weight, SEG)
    spot = jnp.arange(SEG * tokens, dtype=jnp.int32)
    place = (key[:, None] == spot[None, :]).astype(BF)
    high = lax.reduce_precision(weight_line, 8, 7)
    low = weight_line - high
    here = spot[:, None] == key[None, :]
    return (
        place,
        jnp.where(here, high[None, :], 0.0).astype(BF),
        jnp.where(here, low[None, :], 0.0).astype(BF),
    )


def per_device(
    queries,
    cache_keys,
    cache_values,
    new_keys,
    new_values,
    counts,
    lengths,
    residual,
    o_weight,
    norm_gain,
    expert_ids,
    route_weights,
    gate_weight,
    up_weight,
    down_weight,
):
    requests, slots, _ = queries.shape
    rows, width = residual.shape
    experts = math.prod(lax.axis_size(a) for a in AXES)
    attended = attend(queries, cache_keys, cache_values, new_keys, new_values, counts, lengths)
    tokens = lax.all_gather(attended, "y", axis=0, tiled=True)
    place, high, low = routing(expert_ids, route_weights, experts)
    token_index = lax.axis_index("x") * rows + jnp.arange(rows, dtype=jnp.int32)
    count_of = jnp.sum(
        jnp.where(
            (token_index // slots)[:, None] == jnp.arange(requests, dtype=jnp.int32)[None, :],
            counts[None, :],
            0,
        ),
        axis=1,
    )
    live = (token_index % slots < count_of).astype(jnp.int32)[:, None]
    partial, (place, high, low, live) = project(tokens, o_weight, (place, high, low, live))
    partial = partial.reshape(-1, rows, partial.shape[1])
    arrived = lax.all_to_all(partial, ("y", "x"), split_axis=0, concat_axis=0, tiled=True)
    hidden, outgoing = norm_and_place(arrived, residual, norm_gain[None, :], place)
    outgoing = outgoing.reshape(experts, CAP * SEG, width // SEG)
    received = lax.all_to_all(outgoing, AXES, split_axis=0, concat_axis=0, tiled=True)
    results = apply_expert(
        received.reshape(-1, width // SEG), gate_weight[0], up_weight[0], down_weight[0]
    )
    results = results.reshape(experts, CAP * SEG, width // SEG)
    back = lax.all_to_all(results, AXES, split_axis=0, concat_axis=0, tiled=True)
    return combine(back.reshape(-1, width // SEG), high, low, hidden, live)


def solution(mesh):
    fine = Mesh(mesh.devices.reshape(4, 4, 2, 4), AXES)
    req = ("y", "z", "c")
    every = AXES
    return jax.shard_map(
        per_device,
        mesh=fine,
        in_specs=(
            P(req, None, "x"),
            P(req, None, "x"),
            P(req, None, "x"),
            P(req, None, "x"),
            P(req, None, "x"),
            P(req),
            P(req),
            P(every, None),
            P("x", req),
            P(),
            P(every, None),
            P(every, None),
            P(every, None, None),
            P(every, None, None),
            P(every, None, None),
        ),
        out_specs=P(every, None),
        check_vma=False,
    )
```

```python
import functools
import math

import jax
import jax.numpy as jnp
from jax import lax
from jax.experimental import pallas as pl
from jax.experimental.pallas import tpu as pltpu
from jax.sharding import Mesh
from jax.sharding import PartitionSpec as P

HEAD_DIM = 128
TOPK = 8
CAP = 2
LANES = 128
AHEAD = 6
SEG = 4
AXES = ("y", "z", "c", "x")
BF = jnp.bfloat16
F32 = jnp.float32


def dot(a, b):
    return jnp.dot(a, b, preferred_element_type=F32)


def dot_t(a, b):
    return lax.dot_general(a, b, (((1,), (1,)), ((), ())), preferred_element_type=F32)


def vmem(n):
    return [pl.BlockSpec(memory_space=pltpu.VMEM)] * n


def attend_kernel(
    counts_hbm,
    lengths_hbm,
    q_hbm,
    k_hbm,
    v_hbm,
    nk_hbm,
    nv_hbm,
    out_ref,
    counts,
    lengths,
    q_ref,
    k_ref,
    v_ref,
    nk_ref,
    nv_ref,
    sems,
):
    pairs = (
        (q_hbm, q_ref),
        (k_hbm, k_ref),
        (nk_hbm, nk_ref),
        (lengths_hbm, lengths),
        (counts_hbm, counts),
        (v_hbm, v_ref),
        (nv_hbm, nv_ref),
    )
    copies = [pltpu.make_async_copy(a, b, sems.at[i]) for i, (a, b) in enumerate(pairs)]
    for copy in copies:
        copy.start()
    requests, slots, width = q_ref.shape
    heads = width // HEAD_DIM
    cached = k_ref.shape[1]
    rows = heads * slots
    scale = 1.0 / math.sqrt(HEAD_DIM)
    slot = lax.broadcasted_iota(jnp.int32, (rows, slots), 0) % slots
    fresh = lax.broadcasted_iota(jnp.int32, (rows, slots), 1)
    position = lax.broadcasted_iota(jnp.int32, (rows, cached), 1)
    for copy in copies:
        copy.wait()
    for r in range(requests):
        q = jnp.concatenate(
            [q_ref[r, :, h * HEAD_DIM : (h + 1) * HEAD_DIM] for h in range(heads)], axis=0
        )
        old = dot_t(q, k_ref[r]) * scale
        new = dot_t(q, nk_ref[r]) * scale
        old = jnp.where(position < lengths[r], old, -1e30)
        new = jnp.where((fresh <= slot) & (fresh < counts[r]), new, -1e30)
        highest = jnp.maximum(
            jnp.max(old, axis=1, keepdims=True), jnp.max(new, axis=1, keepdims=True)
        )
        old = jnp.exp(old - highest)
        new = jnp.exp(new - highest)
        total = jnp.sum(old, axis=1, keepdims=True) + jnp.sum(new, axis=1, keepdims=True)
        inverse = 1.0 / total
        mixed = dot((old * inverse).astype(BF), v_ref[r]) + dot(
            (new * inverse).astype(BF), nv_ref[r]
        )
        mixed = mixed.astype(BF)
        for h in range(heads):
            out_ref[r * slots : (r + 1) * slots, h * HEAD_DIM : (h + 1) * HEAD_DIM] = mixed[
                h * slots : (h + 1) * slots
            ]


def attend(queries, cache_keys, cache_values, new_keys, new_values, counts, lengths):
    requests, slots, width = queries.shape
    arrays = (queries, cache_keys, cache_values, new_keys, new_values)
    return pl.pallas_call(
        attend_kernel,
        out_shape=jax.ShapeDtypeStruct((requests * slots, width), BF),
        in_specs=[pl.BlockSpec(memory_space=pl.ANY)] * 7,
        out_specs=pl.BlockSpec(memory_space=pltpu.VMEM),
        scratch_shapes=[pltpu.SMEM((requests,), jnp.int32)] * 2
        + [pltpu.VMEM(a.shape, a.dtype) for a in arrays]
        + [pltpu.SemaphoreType.DMA((7,))],
        compiler_params=pltpu.CompilerParams(vmem_limit_bytes=60 << 20),
        cost_estimate=pl.CostEstimate(
            flops=4 * 768 * 544 * 128, bytes_accessed=1 << 20, transcendentals=768 * 544
        ),
        name="attend",
    )(counts, lengths, *arrays)


def project_kernel(homes, near_hbm, across_hbm, *refs):
    pieces, (out_ref, tokens, weight, sems) = refs[:-4], refs[-4:]
    z, zs, c = lax.axis_index("z"), lax.axis_size("z"), lax.axis_index("c")
    part = pieces[0].shape[0]
    rows = near_hbm.shape[0]
    copies = []
    for i, (block, home) in enumerate(((near_hbm, c), (across_hbm, 1 - c))):
        at = pl.ds(pl.multiple_of(home * rows, rows), rows)
        copies.append(pltpu.make_async_copy(block, tokens.at[at, :], sems.at[len(pieces) + i]))
    for i, (piece, back) in enumerate(zip(pieces, homes)):
        home = lax.rem(z + zs - back, zs)
        at = pl.ds(pl.multiple_of(home * part, part), part)
        copies.append(pltpu.make_async_copy(piece, weight.at[at, :], sems.at[i]))
    for copy in copies:
        copy.start()
    for copy in copies:
        copy.wait()
    columns = out_ref.shape[1]
    for j in range(0, columns, 256):
        at = slice(j, min(j + 256, columns))
        out_ref[:, at] = dot_t(tokens[...], weight[at, :]).astype(BF)


def project(attended, o_weight, route):
    zs = lax.axis_size("z")
    own = o_weight.T
    along = [
        lax.ppermute(own, "z", [(i, (i + k) % zs) for i in range(zs)]) for k in range(1, zs)
    ]
    near = lax.all_gather(attended, "y", axis=0, tiled=True)
    across = lax.ppermute(near, "c", [(0, 1), (1, 0)])
    ready = route(near)
    *along, near, across, ready = lax.optimization_barrier((*along, near, across, ready))
    pieces = [own, *along]
    rows = 2 * near.shape[0]
    part, depth = own.shape
    columns = part * zs
    call = pl.pallas_call(
        functools.partial(project_kernel, tuple(range(zs))),
        out_shape=jax.ShapeDtypeStruct((rows, columns), BF),
        in_specs=[pl.BlockSpec(memory_space=pl.ANY)] * (2 + len(pieces)),
        out_specs=pl.BlockSpec(memory_space=pltpu.VMEM),
        scratch_shapes=[
            pltpu.VMEM((rows, depth), BF),
            pltpu.VMEM((columns, depth), BF),
            pltpu.SemaphoreType.DMA((len(pieces) + 2,)),
        ],
        compiler_params=pltpu.CompilerParams(vmem_limit_bytes=60 << 20),
        name="project",
    )
    return call(near, across, *pieces), ready


def norm_kernel(hops, arrived_ref, residual_ref, gain_ref, place_ref, hidden_ref, out_ref):
    groups, splits, halves, rows, parts, part = hops
    width = residual_ref.shape[1]
    square = jnp.zeros((rows, 1), F32)
    span = parts * part
    for g in range(groups):
        sums = []
        for h in range(halves):
            total = jnp.zeros((rows, span), F32)
            for k in range(splits):
                total = total + arrived_ref[(h * groups + g) * splits + k].astype(F32)
            sums.append(total)
        total = jnp.concatenate(
            [sums[h][:, z * part : (z + 1) * part] for z in range(parts) for h in range(halves)],
            axis=1,
        )
        at = slice(g * halves * span, (g + 1) * halves * span)
        total = total + residual_ref[:, at].astype(F32)
        hidden_ref[:, at] = total
        square = square + jnp.sum(total * total, axis=1, keepdims=True)
    factor = lax.rsqrt(square / width + 1e-05)
    seg = width // SEG
    normed = jnp.concatenate(
        [
            (
                hidden_ref[:, s * seg : (s + 1) * seg]
                * factor
                * gain_ref[:, s * seg : (s + 1) * seg]
            ).astype(BF)
            for s in range(SEG)
        ],
        axis=0,
    )
    tile = 256
    for i in range(out_ref.shape[0] // tile):
        at = pl.ds(i * tile, tile)
        out_ref[at, :] = dot(place_ref[at, :], normed).astype(BF)


def norm_and_place(arrived, residual, gain, place):
    rows, width = residual.shape
    ys, xs, cs, zs = (lax.axis_size(a) for a in ("y", "x", "c", "z"))
    hops = (ys, xs, cs, rows, zs, arrived.shape[2] // zs)
    return pl.pallas_call(
        functools.partial(norm_kernel, hops),
        out_shape=(
            jax.ShapeDtypeStruct((rows, width), F32),
            jax.ShapeDtypeStruct((place.shape[0], width // SEG), BF),
        ),
        in_specs=vmem(4),
        out_specs=tuple(vmem(2)),
        compiler_params=pltpu.CompilerParams(vmem_limit_bytes=32 << 20),
        name="norm_place",
    )(arrived, residual, gain, place)


def expert_kernel(
    x_ref, gate_hbm, up_hbm, down_hbm, out_ref, stage, inner, gate, up, down, sems
):
    rows = x_ref.shape[0] // SEG
    seg = x_ref.shape[1]
    lanes = seg // LANES
    copies = []
    for s in range(SEG):
        at = pl.ds(s * seg, seg)
        copies.append(pltpu.make_async_copy(gate_hbm.at[at, :], gate.at[at, :], sems.at[0, s]))
        copies.append(pltpu.make_async_copy(up_hbm.at[at, :], up.at[at, :], sems.at[1, s]))
    for s in range(SEG):
        at = pl.ds(s * seg, seg)
        copies.append(pltpu.make_async_copy(down_hbm.at[:, at], down.at[:, at], sems.at[2, s]))

    def need(i):
        copies[i].wait()
        if i + AHEAD < len(copies):
            copies[i + AHEAD].start()

    for copy in copies[:AHEAD]:
        copy.start()
    tile = 256
    for i in range(x_ref.shape[0] // tile):
        at = pl.ds(i * tile, tile)
        for k in range(lanes):
            stage[k, at, :] = x_ref[at, k * LANES : (k + 1) * LANES].astype(F32)
    gate_sum = up_sum = None
    for s in range(SEG):
        at = pl.ds(s * seg, seg)
        x = jnp.concatenate(
            [stage[k, pl.ds(s, rows, stride=SEG), :].astype(BF) for k in range(lanes)], axis=1
        )
        need(2 * s)
        gate_part = dot(x, gate[at, :])
        need(2 * s + 1)
        up_part = dot(x, up[at, :])
        gate_sum = gate_part if s == 0 else gate_sum + gate_part
        up_sum = up_part if s == 0 else up_sum + up_part
    inner[...] = (gate_sum / (1.0 + jnp.exp(-gate_sum)) * up_sum).astype(BF)
    for s in range(SEG):
        need(2 * SEG + s)
        result = dot(inner[...], down[:, pl.ds(s * seg, seg)])
        for k in range(lanes):
            stage[k, pl.ds(s, rows, stride=SEG), :] = result[:, k * LANES : (k + 1) * LANES]
    for i in range(x_ref.shape[0] // tile):
        at = pl.ds(i * tile, tile)
        for k in range(lanes):
            out_ref[at, k * LANES : (k + 1) * LANES] = stage[k, at, :].astype(BF)


def apply_expert(rows, gate, up, down):
    count, seg = rows.shape
    width, half = gate.shape
    return pl.pallas_call(
        expert_kernel,
        out_shape=jax.ShapeDtypeStruct((count, seg), BF),
        in_specs=vmem(1) + [pl.BlockSpec(memory_space=pl.ANY)] * 3,
        out_specs=pl.BlockSpec(memory_space=pltpu.VMEM),
        scratch_shapes=[
            pltpu.VMEM((seg // LANES, count, LANES), F32),
            pltpu.VMEM((count // SEG, half), BF),
            pltpu.VMEM((width, half), BF),
            pltpu.VMEM((width, half), BF),
            pltpu.VMEM((half, width), BF),
            pltpu.SemaphoreType.DMA((3, SEG)),
        ],
        compiler_params=pltpu.CompilerParams(vmem_limit_bytes=44 << 20),
        name="expert",
    )(rows, gate, up, down)


def combine_kernel(back_ref, shares_ref, hidden_ref, live_ref, out_ref):
    rows, width = hidden_ref.shape
    seg = width // SEG
    half = SEG * rows
    mixed = dot(shares_ref[...], back_ref[...])
    mixed = mixed[:half] + mixed[half:]
    live = live_ref[...] > 0
    for s in range(SEG):
        at = slice(s * seg, (s + 1) * seg)
        total = hidden_ref[:, at] + mixed[s * rows : (s + 1) * rows]
        out_ref[:, at] = jnp.where(live, total, 0.0).astype(BF)


def combine(back, shares, hidden, live):
    return pl.pallas_call(
        combine_kernel,
        out_shape=jax.ShapeDtypeStruct(hidden.shape, BF),
        in_specs=vmem(4),
        out_specs=pl.BlockSpec(memory_space=pltpu.VMEM),
        compiler_params=pltpu.CompilerParams(vmem_limit_bytes=32 << 20),
        name="combine",
    )(back, shares, hidden, live)


def routing(expert_ids, route_weights, experts):
    tokens = expert_ids.shape[0]
    pairs = tokens * TOPK
    destination = expert_ids.reshape(pairs)
    number = jnp.arange(pairs, dtype=jnp.int32)
    earlier = (destination[:, None] == destination[None, :]) & (number[:, None] < number[None, :])
    rank = jnp.sum(earlier.astype(jnp.int32), axis=0)
    slot = destination * CAP + rank
    match = slot[None, :] == jnp.arange(experts * CAP, dtype=jnp.int32)[:, None]
    token = jnp.sum(jnp.where(match, number[None, :] // TOPK + 1, 0), axis=1) - 1
    weight = jnp.sum(jnp.where(match, route_weights.reshape(pairs)[None, :], 0.0), axis=1)
    line = jnp.arange(experts * CAP * SEG, dtype=jnp.int32)
    token_line = jnp.repeat(token, SEG)
    key = jnp.where(token_line < 0, -1, (line % SEG) * tokens + token_line)
    weight_line = jnp.repeat(weight, SEG)
    spot = jnp.arange(SEG * tokens, dtype=jnp.int32)
    place = (key[:, None] == spot[None, :]).astype(BF)
    high = lax.reduce_precision(weight_line, 8, 7)
    low = weight_line - high
    here = spot[:, None] == key[None, :]
    shares = jnp.concatenate(
        [jnp.where(here, part[None, :], 0.0).astype(BF) for part in (high, low)], axis=0
    )
    return place, shares


def per_device(
    queries,
    cache_keys,
    cache_values,
    new_keys,
    new_values,
    counts,
    lengths,
    residual,
    o_weight,
    norm_gain,
    expert_ids,
    route_weights,
    gate_weight,
    up_weight,
    down_weight,
):
    requests, slots, _ = queries.shape
    rows, width = residual.shape
    experts = math.prod(lax.axis_size(a) for a in AXES)
    attended = attend(queries, cache_keys, cache_values, new_keys, new_values, counts, lengths)
    token_index = lax.axis_index("x") * rows + jnp.arange(rows, dtype=jnp.int32)
    count_of = jnp.sum(
        jnp.where(
            (token_index // slots)[:, None] == jnp.arange(requests, dtype=jnp.int32)[None, :],
            counts[None, :],
            0,
        ),
        axis=1,
    )
    live = (token_index % slots < count_of).astype(jnp.int32)[:, None]

    def route(after):
        ids, weights, _ = lax.optimization_barrier((expert_ids, route_weights, after))
        return (*routing(ids, weights, experts), live)

    partial, (place, shares, live) = project(attended, o_weight, route)
    partial = partial.reshape(-1, rows, partial.shape[1])
    arrived = lax.all_to_all(partial, ("c", "y", "x"), split_axis=0, concat_axis=0, tiled=True)
    hidden, outgoing = norm_and_place(arrived, residual, norm_gain[None, :], place)
    outgoing = outgoing.reshape(experts, CAP * SEG, width // SEG)
    received = lax.all_to_all(outgoing, AXES, split_axis=0, concat_axis=0, tiled=True)
    results = apply_expert(
        received.reshape(-1, width // SEG), gate_weight[0], up_weight[0], down_weight[0]
    )
    results = results.reshape(experts, CAP * SEG, width // SEG)
    back = lax.all_to_all(results, AXES, split_axis=0, concat_axis=0, tiled=True)
    return combine(back.reshape(-1, width // SEG), shares, hidden, live)


def solution(mesh):
    fine = Mesh(mesh.devices.reshape(4, 4, 2, 4), AXES)
    req = ("y", "z", "c")
    every = AXES
    return jax.shard_map(
        per_device,
        mesh=fine,
        in_specs=(
            P(req, None, "x"),
            P(req, None, "x"),
            P(req, None, "x"),
            P(req, None, "x"),
            P(req, None, "x"),
            P(req),
            P(req),
            P(every, None),
            P("x", req),
            P(),
            P(every, None),
            P(every, None),
            P(every, None, None),
            P(every, None, None),
            P(every, None, None),
        ),
        out_specs=P(every, None),
        check_vma=False,
    )
```

```python
import functools
import math

import jax
import jax.numpy as jnp
from jax import lax
from jax.experimental import pallas as pl
from jax.experimental.pallas import tpu as pltpu
from jax.sharding import Mesh
from jax.sharding import PartitionSpec as P

HEAD_DIM = 128
TOPK = 8
CAP = 2
LANES = 128
AHEAD = 6
SEG = 4
AXES = ("y", "z", "c", "x")
BF = jnp.bfloat16
F32 = jnp.float32


def dot(a, b):
    return jnp.dot(a, b, preferred_element_type=F32)


def dot_t(a, b):
    return lax.dot_general(a, b, (((1,), (1,)), ((), ())), preferred_element_type=F32)


def vmem(n):
    return [pl.BlockSpec(memory_space=pltpu.VMEM)] * n


def attend_kernel(
    counts_hbm,
    lengths_hbm,
    q_hbm,
    k_hbm,
    v_hbm,
    nk_hbm,
    nv_hbm,
    out_ref,
    counts,
    lengths,
    q_ref,
    k_ref,
    v_ref,
    nk_ref,
    nv_ref,
    sems,
):
    pairs = (
        (q_hbm, q_ref),
        (k_hbm, k_ref),
        (nk_hbm, nk_ref),
        (lengths_hbm, lengths),
        (counts_hbm, counts),
        (v_hbm, v_ref),
        (nv_hbm, nv_ref),
    )
    copies = [pltpu.make_async_copy(a, b, sems.at[i]) for i, (a, b) in enumerate(pairs)]
    for copy in copies:
        copy.start()
    requests, slots, width = q_ref.shape
    heads = width // HEAD_DIM
    cached = k_ref.shape[1]
    rows = heads * slots
    scale = 1.0 / math.sqrt(HEAD_DIM)
    slot = lax.broadcasted_iota(jnp.int32, (rows, slots), 0) % slots
    fresh = lax.broadcasted_iota(jnp.int32, (rows, slots), 1)
    position = lax.broadcasted_iota(jnp.int32, (rows, cached), 1)
    for copy in copies[:5]:
        copy.wait()
    for r in range(requests):
        q = jnp.concatenate(
            [q_ref[r, :, h * HEAD_DIM : (h + 1) * HEAD_DIM] for h in range(heads)], axis=0
        )
        old = dot_t(q, k_ref[r]) * scale
        new = dot_t(q, nk_ref[r]) * scale
        old = jnp.where(position < lengths[r], old, -1e30)
        new = jnp.where((fresh <= slot) & (fresh < counts[r]), new, -1e30)
        highest = jnp.maximum(
            jnp.max(old, axis=1, keepdims=True), jnp.max(new, axis=1, keepdims=True)
        )
        old = jnp.exp(old - highest)
        new = jnp.exp(new - highest)
        total = jnp.sum(old, axis=1, keepdims=True) + jnp.sum(new, axis=1, keepdims=True)
        inverse = 1.0 / total
        if r == 0:
            for copy in copies[5:]:
                copy.wait()
        mixed = dot((old * inverse).astype(BF), v_ref[r]) + dot(
            (new * inverse).astype(BF), nv_ref[r]
        )
        mixed = mixed.astype(BF)
        for h in range(heads):
            out_ref[r * slots : (r + 1) * slots, h * HEAD_DIM : (h + 1) * HEAD_DIM] = mixed[
                h * slots : (h + 1) * slots
            ]


def attend(queries, cache_keys, cache_values, new_keys, new_values, counts, lengths):
    requests, slots, width = queries.shape
    arrays = (queries, cache_keys, cache_values, new_keys, new_values)
    return pl.pallas_call(
        attend_kernel,
        out_shape=jax.ShapeDtypeStruct((requests * slots, width), BF),
        in_specs=[pl.BlockSpec(memory_space=pl.ANY)] * 7,
        out_specs=pl.BlockSpec(memory_space=pltpu.VMEM),
        scratch_shapes=[pltpu.SMEM((requests,), jnp.int32)] * 2
        + [pltpu.VMEM(a.shape, a.dtype) for a in arrays]
        + [pltpu.SemaphoreType.DMA((7,))],
        compiler_params=pltpu.CompilerParams(vmem_limit_bytes=60 << 20),
        cost_estimate=pl.CostEstimate(
            flops=4 * 768 * 544 * 128, bytes_accessed=1 << 20, transcendentals=768 * 544
        ),
        name="attend",
    )(counts, lengths, *arrays)


def project_kernel(homes, near_ref, across_ref, *refs):
    pieces, (out_ref, weight, sems) = refs[:-3], refs[-3:]
    z, zs, c = lax.axis_index("z"), lax.axis_size("z"), lax.axis_index("c")
    part = pieces[0].shape[0]
    rows = near_ref.shape[0]
    copies = []
    for i, (piece, back) in enumerate(zip(pieces, homes)):
        home = lax.rem(z + zs - back, zs)
        at = pl.ds(pl.multiple_of(home * part, part), part)
        copies.append(pltpu.make_async_copy(piece, weight.at[at, :], sems.at[i]))
    for copy in copies:
        copy.start()
    for copy in copies:
        copy.wait()
    columns = out_ref.shape[1]
    for j in range(0, columns, 256):
        at = slice(j, min(j + 256, columns))
        for block, home in ((near_ref, c), (across_ref, 1 - c)):
            out_ref[pl.ds(pl.multiple_of(home * rows, rows), rows), at] = dot_t(
                block[...], weight[at, :]
            ).astype(BF)


def project(attended, own, route):
    zs = lax.axis_size("z")
    along = [
        lax.ppermute(own, "z", [(i, (i + k) % zs) for i in range(zs)]) for k in range(1, zs)
    ]
    near = lax.all_gather(attended, "y", axis=0, tiled=True)
    across = lax.ppermute(near, "c", [(0, 1), (1, 0)])
    ready = route(near)
    *along, near, across, ready = lax.optimization_barrier((*along, near, across, ready))
    pieces = [own, *along]
    rows = 2 * near.shape[0]
    part, depth = own.shape
    columns = part * zs
    call = pl.pallas_call(
        functools.partial(project_kernel, tuple(range(zs))),
        out_shape=jax.ShapeDtypeStruct((rows, columns), BF),
        in_specs=vmem(2) + [pl.BlockSpec(memory_space=pl.ANY)] * len(pieces),
        out_specs=pl.BlockSpec(memory_space=pltpu.VMEM),
        scratch_shapes=[
            pltpu.VMEM((columns, depth), BF),
            pltpu.SemaphoreType.DMA((len(pieces),)),
        ],
        compiler_params=pltpu.CompilerParams(vmem_limit_bytes=16 << 20),
        name="project",
    )
    return call(near, across, *pieces), ready


def norm_kernel(hops, arrived_ref, residual_ref, gain_ref, place_ref, hidden_ref, out_ref):
    groups, splits, halves, rows, parts, part = hops
    width = residual_ref.shape[1]
    square = jnp.zeros((rows, 1), F32)
    span = parts * part
    for g in range(groups):
        sums = []
        for h in range(halves):
            total = jnp.zeros((rows, span), F32)
            for k in range(splits):
                total = total + arrived_ref[(h * groups + g) * splits + k].astype(F32)
            sums.append(total)
        total = jnp.concatenate(
            [sums[h][:, z * part : (z + 1) * part] for z in range(parts) for h in range(halves)],
            axis=1,
        )
        at = slice(g * halves * span, (g + 1) * halves * span)
        total = total + residual_ref[:, at].astype(F32)
        hidden_ref[:, at] = total
        square = square + jnp.sum(total * total, axis=1, keepdims=True)
    factor = lax.rsqrt(square / width + 1e-05)
    seg = width // SEG
    normed = jnp.concatenate(
        [
            (
                hidden_ref[:, s * seg : (s + 1) * seg]
                * factor
                * gain_ref[:, s * seg : (s + 1) * seg]
            ).astype(BF)
            for s in range(SEG)
        ],
        axis=0,
    )
    tile = 256
    for i in range(out_ref.shape[0] // tile):
        at = pl.ds(i * tile, tile)
        out_ref[at, :] = dot(place_ref[at, :], normed).astype(BF)


def norm_and_place(arrived, residual, gain, place):
    rows, width = residual.shape
    ys, xs, cs, zs = (lax.axis_size(a) for a in ("y", "x", "c", "z"))
    hops = (ys, xs, cs, rows, zs, arrived.shape[2] // zs)
    return pl.pallas_call(
        functools.partial(norm_kernel, hops),
        out_shape=(
            jax.ShapeDtypeStruct((rows, width), F32),
            jax.ShapeDtypeStruct((place.shape[0], width // SEG), BF),
        ),
        in_specs=vmem(4),
        out_specs=tuple(vmem(2)),
        compiler_params=pltpu.CompilerParams(vmem_limit_bytes=32 << 20),
        name="norm_place",
    )(arrived, residual, gain, place)


def expert_kernel(
    x_ref, gate_hbm, up_hbm, down_hbm, out_ref, stage, inner, gate, up, down, sems
):
    rows = x_ref.shape[0] // SEG
    seg = x_ref.shape[1]
    lanes = seg // LANES
    copies = []
    for s in range(SEG):
        at = pl.ds(s * seg, seg)
        copies.append(pltpu.make_async_copy(gate_hbm.at[at, :], gate.at[at, :], sems.at[0, s]))
        copies.append(pltpu.make_async_copy(up_hbm.at[at, :], up.at[at, :], sems.at[1, s]))
    part = down.shape[0] // SEG
    for s in range(SEG):
        at = pl.ds(s * part, part)
        copies.append(pltpu.make_async_copy(down_hbm.at[at, :], down.at[at, :], sems.at[2, s]))

    def need(i):
        copies[i].wait()
        if i + AHEAD < len(copies):
            copies[i + AHEAD].start()

    for copy in copies[:AHEAD]:
        copy.start()
    tile = 256
    for i in range(x_ref.shape[0] // tile):
        at = pl.ds(i * tile, tile)
        for k in range(lanes):
            stage[k, at, :] = x_ref[at, k * LANES : (k + 1) * LANES].astype(F32)
    gate_sum = up_sum = None
    for s in range(SEG):
        at = pl.ds(s * seg, seg)
        x = jnp.concatenate(
            [stage[k, pl.ds(s, rows, stride=SEG), :].astype(BF) for k in range(lanes)], axis=1
        )
        need(2 * s)
        gate_part = dot(x, gate[at, :])
        need(2 * s + 1)
        up_part = dot(x, up[at, :])
        gate_sum = gate_part if s == 0 else gate_sum + gate_part
        up_sum = up_part if s == 0 else up_sum + up_part
    inner[...] = (gate_sum / (1.0 + jnp.exp(-gate_sum)) * up_sum).astype(BF)
    for s in range(SEG):
        need(2 * SEG + s)
    for s in range(SEG):
        result = dot(inner[...], down[:, pl.ds(s * seg, seg)])
        for k in range(lanes):
            stage[k, pl.ds(s, rows, stride=SEG), :] = result[:, k * LANES : (k + 1) * LANES]
    for i in range(x_ref.shape[0] // tile):
        at = pl.ds(i * tile, tile)
        for k in range(lanes):
            out_ref[at, k * LANES : (k + 1) * LANES] = stage[k, at, :].astype(BF)


def apply_expert(rows, gate, up, down):
    count, seg = rows.shape
    width, half = gate.shape
    return pl.pallas_call(
        expert_kernel,
        out_shape=jax.ShapeDtypeStruct((count, seg), BF),
        in_specs=vmem(1) + [pl.BlockSpec(memory_space=pl.ANY)] * 3,
        out_specs=pl.BlockSpec(memory_space=pltpu.VMEM),
        scratch_shapes=[
            pltpu.VMEM((seg // LANES, count, LANES), F32),
            pltpu.VMEM((count // SEG, half), BF),
            pltpu.VMEM((width, half), BF),
            pltpu.VMEM((width, half), BF),
            pltpu.VMEM((half, width), BF),
            pltpu.SemaphoreType.DMA((3, SEG)),
        ],
        compiler_params=pltpu.CompilerParams(vmem_limit_bytes=44 << 20),
        name="expert",
    )(rows, gate, up, down)


def combine_kernel(back_ref, shares_ref, hidden_ref, live_ref, out_ref):
    rows, width = hidden_ref.shape
    seg = width // SEG
    half = SEG * rows
    mixed = dot(shares_ref[...], back_ref[...])
    mixed = mixed[:half] + mixed[half:]
    live = live_ref[...] > 0
    for s in range(SEG):
        at = slice(s * seg, (s + 1) * seg)
        total = hidden_ref[:, at] + mixed[s * rows : (s + 1) * rows]
        out_ref[:, at] = jnp.where(live, total, 0.0).astype(BF)


def combine(back, shares, hidden, live):
    return pl.pallas_call(
        combine_kernel,
        out_shape=jax.ShapeDtypeStruct(hidden.shape, BF),
        in_specs=vmem(4),
        out_specs=pl.BlockSpec(memory_space=pltpu.VMEM),
        compiler_params=pltpu.CompilerParams(vmem_limit_bytes=32 << 20),
        name="combine",
    )(back, shares, hidden, live)


def routing(expert_ids, route_weights, experts):
    tokens = expert_ids.shape[0]
    pairs = tokens * TOPK
    destination = expert_ids.reshape(pairs)
    number = jnp.arange(pairs, dtype=jnp.int32)
    earlier = (destination[:, None] == destination[None, :]) & (number[:, None] < number[None, :])
    rank = jnp.sum(earlier.astype(jnp.int32), axis=0)
    slot = destination * CAP + rank
    match = slot[None, :] == jnp.arange(experts * CAP, dtype=jnp.int32)[:, None]
    token = jnp.sum(jnp.where(match, number[None, :] // TOPK + 1, 0), axis=1) - 1
    weight = jnp.sum(jnp.where(match, route_weights.reshape(pairs)[None, :], 0.0), axis=1)
    line = jnp.arange(experts * CAP * SEG, dtype=jnp.int32)
    token_line = jnp.repeat(token, SEG)
    key = jnp.where(token_line < 0, -1, (line % SEG) * tokens + token_line)
    weight_line = jnp.repeat(weight, SEG)
    spot = jnp.arange(SEG * tokens, dtype=jnp.int32)
    place = (key[:, None] == spot[None, :]).astype(BF)
    high = lax.reduce_precision(weight_line, 8, 7)
    low = weight_line - high
    here = spot[:, None] == key[None, :]
    shares = jnp.concatenate(
        [jnp.where(here, part[None, :], 0.0).astype(BF) for part in (high, low)], axis=0
    )
    return place, shares


def per_device(
    queries,
    cache_keys,
    cache_values,
    new_keys,
    new_values,
    counts,
    lengths,
    residual,
    o_weight,
    norm_gain,
    expert_ids,
    route_weights,
    gate_weight,
    up_weight,
    down_weight,
):
    requests, slots, _ = queries.shape
    rows, width = residual.shape
    experts = math.prod(lax.axis_size(a) for a in AXES)
    attended = attend(queries, cache_keys, cache_values, new_keys, new_values, counts, lengths)
    token_index = lax.axis_index("x") * rows + jnp.arange(rows, dtype=jnp.int32)
    count_of = jnp.sum(
        jnp.where(
            (token_index // slots)[:, None] == jnp.arange(requests, dtype=jnp.int32)[None, :],
            counts[None, :],
            0,
        ),
        axis=1,
    )
    live = (token_index % slots < count_of).astype(jnp.int32)[:, None]

    def route(after):
        ids, weights, _ = lax.optimization_barrier((expert_ids, route_weights, after))
        return (*routing(ids, weights, experts), live)

    partial, (place, shares, live) = project(attended, o_weight.T, route)
    partial = partial.reshape(-1, rows, partial.shape[1])
    arrived = lax.all_to_all(partial, ("c", "y", "x"), split_axis=0, concat_axis=0, tiled=True)
    hidden, outgoing = norm_and_place(arrived, residual, norm_gain[None, :], place)
    outgoing = outgoing.reshape(experts, CAP * SEG, width // SEG)
    received = lax.all_to_all(outgoing, AXES, split_axis=0, concat_axis=0, tiled=True)
    results = apply_expert(
        received.reshape(-1, width // SEG), gate_weight[0], up_weight[0], down_weight[0]
    )
    results = results.reshape(experts, CAP * SEG, width // SEG)
    back = lax.all_to_all(results, AXES, split_axis=0, concat_axis=0, tiled=True)
    return combine(back.reshape(-1, width // SEG), shares, hidden, live)


def solution(mesh):
    fine = Mesh(mesh.devices.reshape(4, 4, 2, 4), AXES)
    req = ("y", "z", "c")
    every = AXES
    return jax.shard_map(
        per_device,
        mesh=fine,
        in_specs=(
            P(req, None, "x"),
            P(req, None, "x"),
            P(req, None, "x"),
            P(req, None, "x"),
            P(req, None, "x"),
            P(req),
            P(req),
            P(every, None),
            P("x", req),
            P(),
            P(every, None),
            P(every, None),
            P(every, None, None),
            P(every, None, None),
            P(every, None, None),
        ),
        out_specs=P(every, None),
        check_vma=False,
    )
```

```python
import functools
import math

import jax
import jax.numpy as jnp
from jax import lax
from jax.experimental import pallas as pl
from jax.experimental.pallas import tpu as pltpu
from jax.sharding import Mesh
from jax.sharding import PartitionSpec as P

HEAD_DIM = 128
TOPK = 8
CAP = 2
LANES = 128
AHEAD = 6
SEG = 4
AXES = ("y", "z", "c", "x")
BF = jnp.bfloat16
F32 = jnp.float32


def dot(a, b):
    return jnp.dot(a, b, preferred_element_type=F32)


def dot_t(a, b):
    return lax.dot_general(a, b, (((1,), (1,)), ((), ())), preferred_element_type=F32)


def vmem(n):
    return [pl.BlockSpec(memory_space=pltpu.VMEM)] * n


def attend_kernel(
    counts_hbm,
    lengths_hbm,
    q_hbm,
    k_hbm,
    v_hbm,
    nk_hbm,
    nv_hbm,
    out_ref,
    counts,
    lengths,
    q_ref,
    k_ref,
    v_ref,
    nk_ref,
    nv_ref,
    sems,
):
    pairs = (
        (q_hbm, q_ref),
        (k_hbm, k_ref),
        (nk_hbm, nk_ref),
        (lengths_hbm, lengths),
        (counts_hbm, counts),
        (v_hbm, v_ref),
        (nv_hbm, nv_ref),
    )
    copies = [pltpu.make_async_copy(a, b, sems.at[i]) for i, (a, b) in enumerate(pairs)]
    for copy in copies:
        copy.start()
    requests, slots, width = q_ref.shape
    heads = width // HEAD_DIM
    cached = k_ref.shape[1]
    rows = heads * slots
    scale = 1.0 / math.sqrt(HEAD_DIM)
    slot = lax.broadcasted_iota(jnp.int32, (rows, slots), 0) % slots
    fresh = lax.broadcasted_iota(jnp.int32, (rows, slots), 1)
    position = lax.broadcasted_iota(jnp.int32, (rows, cached), 1)
    for copy in copies[:5]:
        copy.wait()
    for r in range(requests):
        q = jnp.concatenate(
            [q_ref[r, :, h * HEAD_DIM : (h + 1) * HEAD_DIM] for h in range(heads)], axis=0
        )
        old = dot_t(q, k_ref[r]) * scale
        new = dot_t(q, nk_ref[r]) * scale
        old = jnp.where(position < lengths[r], old, -1e30)
        new = jnp.where((fresh <= slot) & (fresh < counts[r]), new, -1e30)
        highest = jnp.maximum(
            jnp.max(old, axis=1, keepdims=True), jnp.max(new, axis=1, keepdims=True)
        )
        old = jnp.exp(old - highest)
        new = jnp.exp(new - highest)
        total = jnp.sum(old, axis=1, keepdims=True) + jnp.sum(new, axis=1, keepdims=True)
        inverse = 1.0 / total
        if r == 0:
            for copy in copies[5:]:
                copy.wait()
        mixed = dot((old * inverse).astype(BF), v_ref[r]) + dot(
            (new * inverse).astype(BF), nv_ref[r]
        )
        mixed = mixed.astype(BF)
        for h in range(heads):
            out_ref[r * slots : (r + 1) * slots, h * HEAD_DIM : (h + 1) * HEAD_DIM] = mixed[
                h * slots : (h + 1) * slots
            ]


def attend(queries, cache_keys, cache_values, new_keys, new_values, counts, lengths):
    requests, slots, width = queries.shape
    arrays = (queries, cache_keys, cache_values, new_keys, new_values)
    return pl.pallas_call(
        attend_kernel,
        out_shape=jax.ShapeDtypeStruct((requests * slots, width), BF),
        in_specs=[pl.BlockSpec(memory_space=pl.ANY)] * 7,
        out_specs=pl.BlockSpec(memory_space=pltpu.VMEM),
        scratch_shapes=[pltpu.SMEM((requests,), jnp.int32)] * 2
        + [pltpu.VMEM(a.shape, a.dtype) for a in arrays]
        + [pltpu.SemaphoreType.DMA((7,))],
        compiler_params=pltpu.CompilerParams(vmem_limit_bytes=60 << 20),
        cost_estimate=pl.CostEstimate(
            flops=4 * 768 * 544 * 128, bytes_accessed=1 << 20, transcendentals=768 * 544
        ),
        name="attend",
    )(counts, lengths, *arrays)


def project_kernel(homes, near_ref, across_ref, *refs):
    pieces, (out_ref, weight, sems) = refs[:-3], refs[-3:]
    z, zs, c = lax.axis_index("z"), lax.axis_size("z"), lax.axis_index("c")
    part = pieces[0].shape[0]
    rows = near_ref.shape[0]
    copies = []
    for i, (piece, back) in enumerate(zip(pieces, homes)):
        home = lax.rem(z + zs - back, zs)
        at = pl.ds(pl.multiple_of(home * part, part), part)
        copies.append(pltpu.make_async_copy(piece, weight.at[at, :], sems.at[i]))
    for copy in copies:
        copy.start()
    for copy in copies:
        copy.wait()
    columns = out_ref.shape[1]
    for j in range(0, columns, 256):
        at = slice(j, min(j + 256, columns))
        for block, home in ((near_ref, c), (across_ref, 1 - c)):
            out_ref[pl.ds(pl.multiple_of(home * rows, rows), rows), at] = dot_t(
                block[...], weight[at, :]
            ).astype(BF)


def project(attended, own, route):
    zs = lax.axis_size("z")
    along = [
        lax.ppermute(own, "z", [(i, (i + k) % zs) for i in range(zs)]) for k in (1, 3, 2)
    ]
    near = lax.all_gather(attended, "y", axis=0, tiled=True)
    across = lax.ppermute(near, "c", [(0, 1), (1, 0)])
    ready = route(near)
    *along, near, across, ready = lax.optimization_barrier((*along, near, across, ready))
    pieces = [own, *along]
    rows = 2 * near.shape[0]
    part, depth = own.shape
    columns = part * zs
    call = pl.pallas_call(
        functools.partial(project_kernel, (0, 1, 3, 2)),
        out_shape=jax.ShapeDtypeStruct((rows, columns), BF),
        in_specs=vmem(2) + [pl.BlockSpec(memory_space=pl.ANY)] * len(pieces),
        out_specs=pl.BlockSpec(memory_space=pltpu.VMEM),
        scratch_shapes=[
            pltpu.VMEM((columns, depth), BF),
            pltpu.SemaphoreType.DMA((len(pieces),)),
        ],
        compiler_params=pltpu.CompilerParams(vmem_limit_bytes=16 << 20),
        name="project",
    )
    return call(near, across, *pieces), ready


def norm_kernel(hops, arrived_ref, residual_ref, gain_ref, place_ref, hidden_ref, out_ref):
    groups, splits, halves, rows, parts, part = hops
    width = residual_ref.shape[1]
    square = jnp.zeros((rows, 1), F32)
    span = parts * part
    for g in range(groups):
        sums = []
        for h in range(halves):
            total = jnp.zeros((rows, span), F32)
            for k in range(splits):
                total = total + arrived_ref[(h * groups + g) * splits + k].astype(F32)
            sums.append(total)
        total = jnp.concatenate(
            [sums[h][:, z * part : (z + 1) * part] for z in range(parts) for h in range(halves)],
            axis=1,
        )
        at = slice(g * halves * span, (g + 1) * halves * span)
        total = total + residual_ref[:, at].astype(F32)
        hidden_ref[:, at] = total
        square = square + jnp.sum(total * total, axis=1, keepdims=True)
    factor = lax.rsqrt(square / width + 1e-05)
    seg = width // SEG
    normed = jnp.concatenate(
        [
            (
                hidden_ref[:, s * seg : (s + 1) * seg]
                * factor
                * gain_ref[:, s * seg : (s + 1) * seg]
            ).astype(BF)
            for s in range(SEG)
        ],
        axis=0,
    )
    tile = 256
    for i in range(out_ref.shape[0] // tile):
        at = pl.ds(i * tile, tile)
        out_ref[at, :] = dot(place_ref[at, :], normed).astype(BF)


def norm_and_place(arrived, residual, gain, place):
    rows, width = residual.shape
    ys, xs, cs, zs = (lax.axis_size(a) for a in ("y", "x", "c", "z"))
    hops = (ys, xs, cs, rows, zs, arrived.shape[2] // zs)
    return pl.pallas_call(
        functools.partial(norm_kernel, hops),
        out_shape=(
            jax.ShapeDtypeStruct((rows, width), F32),
            jax.ShapeDtypeStruct((place.shape[0], width // SEG), BF),
        ),
        in_specs=vmem(4),
        out_specs=tuple(vmem(2)),
        compiler_params=pltpu.CompilerParams(vmem_limit_bytes=32 << 20),
        name="norm_place",
    )(arrived, residual, gain, place)


def expert_kernel(
    x_ref, gate_hbm, up_hbm, down_hbm, out_ref, stage, inner, gate, up, down, sems
):
    rows = x_ref.shape[0] // SEG
    seg = x_ref.shape[1]
    lanes = seg // LANES
    copies = []
    for s in range(SEG):
        at = pl.ds(s * seg, seg)
        copies.append(pltpu.make_async_copy(gate_hbm.at[at, :], gate.at[at, :], sems.at[0, s]))
        copies.append(pltpu.make_async_copy(up_hbm.at[at, :], up.at[at, :], sems.at[1, s]))
    part = down.shape[0] // SEG
    for s in range(SEG):
        at = pl.ds(s * part, part)
        copies.append(pltpu.make_async_copy(down_hbm.at[at, :], down.at[at, :], sems.at[2, s]))

    def need(i):
        copies[i].wait()
        if i + AHEAD < len(copies):
            copies[i + AHEAD].start()

    for copy in copies[:AHEAD]:
        copy.start()
    tile = 256
    for i in range(x_ref.shape[0] // tile):
        at = pl.ds(i * tile, tile)
        for k in range(lanes):
            stage[k, at, :] = x_ref[at, k * LANES : (k + 1) * LANES].astype(F32)
    gate_sum = up_sum = None
    for s in range(SEG):
        at = pl.ds(s * seg, seg)
        x = jnp.concatenate(
            [stage[k, pl.ds(s, rows, stride=SEG), :].astype(BF) for k in range(lanes)], axis=1
        )
        need(2 * s)
        gate_part = dot(x, gate[at, :])
        need(2 * s + 1)
        up_part = dot(x, up[at, :])
        gate_sum = gate_part if s == 0 else gate_sum + gate_part
        up_sum = up_part if s == 0 else up_sum + up_part
    inner[...] = (gate_sum / (1.0 + jnp.exp(-gate_sum)) * up_sum).astype(BF)
    for s in range(SEG):
        need(2 * SEG + s)
    for s in range(SEG):
        result = dot(inner[...], down[:, pl.ds(s * seg, seg)])
        for k in range(lanes):
            stage[k, pl.ds(s, rows, stride=SEG), :] = result[:, k * LANES : (k + 1) * LANES]
    for i in range(x_ref.shape[0] // tile):
        at = pl.ds(i * tile, tile)
        for k in range(lanes):
            out_ref[at, k * LANES : (k + 1) * LANES] = stage[k, at, :].astype(BF)


def apply_expert(rows, gate, up, down):
    count, seg = rows.shape
    width, half = gate.shape
    return pl.pallas_call(
        expert_kernel,
        out_shape=jax.ShapeDtypeStruct((count, seg), BF),
        in_specs=vmem(1) + [pl.BlockSpec(memory_space=pl.ANY)] * 3,
        out_specs=pl.BlockSpec(memory_space=pltpu.VMEM),
        scratch_shapes=[
            pltpu.VMEM((seg // LANES, count, LANES), F32),
            pltpu.VMEM((count // SEG, half), BF),
            pltpu.VMEM((width, half), BF),
            pltpu.VMEM((width, half), BF),
            pltpu.VMEM((half, width), BF),
            pltpu.SemaphoreType.DMA((3, SEG)),
        ],
        compiler_params=pltpu.CompilerParams(vmem_limit_bytes=44 << 20),
        name="expert",
    )(rows, gate, up, down)


def combine_kernel(back_ref, shares_ref, hidden_ref, live_ref, out_ref):
    rows, width = hidden_ref.shape
    seg = width // SEG
    half = SEG * rows
    mixed = dot(shares_ref[...], back_ref[...])
    mixed = mixed[:half] + mixed[half:]
    live = live_ref[...] > 0
    for s in range(SEG):
        at = slice(s * seg, (s + 1) * seg)
        total = hidden_ref[:, at] + mixed[s * rows : (s + 1) * rows]
        out_ref[:, at] = jnp.where(live, total, 0.0).astype(BF)


def combine(back, shares, hidden, live):
    return pl.pallas_call(
        combine_kernel,
        out_shape=jax.ShapeDtypeStruct(hidden.shape, BF),
        in_specs=vmem(4),
        out_specs=pl.BlockSpec(memory_space=pltpu.VMEM),
        compiler_params=pltpu.CompilerParams(vmem_limit_bytes=32 << 20),
        name="combine",
    )(back, shares, hidden, live)


def routing(expert_ids, route_weights, experts):
    tokens = expert_ids.shape[0]
    pairs = tokens * TOPK
    destination = expert_ids.reshape(pairs)
    number = jnp.arange(pairs, dtype=jnp.int32)
    earlier = (destination[:, None] == destination[None, :]) & (number[:, None] < number[None, :])
    rank = jnp.sum(earlier.astype(jnp.int32), axis=0)
    slot = destination * CAP + rank
    match = slot[None, :] == jnp.arange(experts * CAP, dtype=jnp.int32)[:, None]
    token = jnp.sum(jnp.where(match, number[None, :] // TOPK + 1, 0), axis=1) - 1
    weight = jnp.sum(jnp.where(match, route_weights.reshape(pairs)[None, :], 0.0), axis=1)
    line = jnp.arange(experts * CAP * SEG, dtype=jnp.int32)
    token_line = jnp.repeat(token, SEG)
    key = jnp.where(token_line < 0, -1, (line % SEG) * tokens + token_line)
    weight_line = jnp.repeat(weight, SEG)
    spot = jnp.arange(SEG * tokens, dtype=jnp.int32)
    place = (key[:, None] == spot[None, :]).astype(BF)
    high = lax.reduce_precision(weight_line, 8, 7)
    low = weight_line - high
    here = spot[:, None] == key[None, :]
    shares = jnp.concatenate(
        [jnp.where(here, part[None, :], 0.0).astype(BF) for part in (high, low)], axis=0
    )
    return place, shares


def per_device(
    queries,
    cache_keys,
    cache_values,
    new_keys,
    new_values,
    counts,
    lengths,
    residual,
    o_weight,
    norm_gain,
    expert_ids,
    route_weights,
    gate_weight,
    up_weight,
    down_weight,
):
    requests, slots, _ = queries.shape
    rows, width = residual.shape
    experts = math.prod(lax.axis_size(a) for a in AXES)
    attended = attend(queries, cache_keys, cache_values, new_keys, new_values, counts, lengths)
    token_index = lax.axis_index("x") * rows + jnp.arange(rows, dtype=jnp.int32)
    count_of = jnp.sum(
        jnp.where(
            (token_index // slots)[:, None] == jnp.arange(requests, dtype=jnp.int32)[None, :],
            counts[None, :],
            0,
        ),
        axis=1,
    )
    live = (token_index % slots < count_of).astype(jnp.int32)[:, None]

    def route(after):
        ids, weights, _ = lax.optimization_barrier((expert_ids, route_weights, after))
        return (*routing(ids, weights, experts), live)

    partial, (place, shares, live) = project(attended, o_weight.T, route)
    partial = partial.reshape(-1, rows, partial.shape[1])
    arrived = lax.all_to_all(partial, ("c", "y", "x"), split_axis=0, concat_axis=0, tiled=True)
    hidden, outgoing = norm_and_place(arrived, residual, norm_gain[None, :], place)
    outgoing = outgoing.reshape(experts, CAP * SEG, width // SEG)
    received = lax.all_to_all(outgoing, AXES, split_axis=0, concat_axis=0, tiled=True)
    results = apply_expert(
        received.reshape(-1, width // SEG), gate_weight[0], up_weight[0], down_weight[0]
    )
    results = results.reshape(experts, CAP * SEG, width // SEG)
    back = lax.all_to_all(results, AXES, split_axis=0, concat_axis=0, tiled=True)
    return combine(back.reshape(-1, width // SEG), shares, hidden, live)


def solution(mesh):
    fine = Mesh(mesh.devices.reshape(4, 4, 2, 4), AXES)
    req = ("y", "z", "c")
    every = AXES
    return jax.shard_map(
        per_device,
        mesh=fine,
        in_specs=(
            P(req, None, "x"),
            P(req, None, "x"),
            P(req, None, "x"),
            P(req, None, "x"),
            P(req, None, "x"),
            P(req),
            P(req),
            P(every, None),
            P("x", req),
            P(),
            P(every, None),
            P(every, None),
            P(every, None, None),
            P(every, None, None),
            P(every, None, None),
        ),
        out_specs=P(every, None),
        check_vma=False,
    )
```
